32 devices in a mesh: groups: 2 (over x), sector: 16 (over z, y, core).
Axes of the slice: x: 2, y: 2, z: 4, core: 2. Of those that a mesh axis runs over, the one named last changes fastest.
Arguments:
- field: float32 [4, 8, 64, 256], P('groups', None, 'sector'), parts along dimension 0, may hold values from -6 to 6
- source: float32 [4, 8, 64, 256], P('groups', None, 'sector'), parts along dimension 0, may hold values from -6 to 6
- materials: int32 [4, 8, 64, 256], P('groups', None, 'sector'), parts along dimension 0, may hold values from 0 to 3
- incoming: float32 [4, 4, 64, 256], P('groups', None, 'sector'), parts along dimension 0, may hold values from -6 to 6
- waveform: float32 [8], P('groups'), parts along dimension 0, may hold values from -1 to 1
- degrees: int32 [8], P('groups'), parts along dimension 0, may hold values from 4 to 8, as said below
- offsets: int32 [8], P('groups'), parts along dimension 0, may hold values from 0 to 15
- conduct: float32 [4], replicated, may hold values from 0.05 to 0.5
- reluct: float32 [4], replicated, may hold values from 0.3 to 3
- robin: float32 [2], replicated, may hold values from 0.5 to 2
Outputs:
- field_end: float32 [4, 8, 64, 256], P('groups', None, 'sector'), parts along dimension 0
- next_incoming: float32 [4, 4, 64, 256], P('groups', None, 'sector'), parts along dimension 0
The draws below stay inside these ranges and needn't reach their ends.
There are 2 independent parts, one for each index of `groups`. The reference program is written for one: setup_inputs(seed, part) draws one part's arguments, and reference() takes and returns one part's arrays. A program takes and returns all parts, laid end to end along the dimension named above; an argument that names none is the same for every part. Nothing has to cross between parts.
Inputs may be any that keep to these rules, and one draw needn't show every extreme that they name: `degrees`: some step of each window has degree 8.
All inputs are finite; a program needn't handle non-finite values.
Results may differ from the reference program's by a relative error of at most 0.000021.
Values sent between devices are 32-bit elements; how exact they have to be, the bound alone decides.
A program may use at most 64 MiB of HBM per device.

```python
import math
import jax
import jax.numpy as jnp
from jax import lax

R = 8
A_DEV = 4
Z = 256
STEPS = 4
DEG = 8
MATS = 4
SECTORS = 16
NA = 64


def draw_degrees(key, part):
    key = jax.random.fold_in(key, 11)
    first_key, second_key = jax.random.split(key)
    values = jax.random.randint(first_key, (STEPS,), DEG // 2, DEG + 1)
    where_top = jax.random.randint(second_key, (), 0, STEPS)
    return jnp.where(jnp.arange(STEPS) == where_top, DEG, values).astype(jnp.int32)


def with_ends(entries, own_key, low, largest):
    dims = entries.shape
    index_at = [jax.random.randint(jax.random.fold_in(own_key, axis), (), 0, dims[axis]) for axis in range(len(dims))]
    entries = entries.at[tuple(index_at)].set(low)
    longest = dims.index(max(dims))
    index_at[longest] = (index_at[longest] + 1) % dims[longest]
    return entries.at[tuple(index_at)].set(largest)


def level_of(stream_key, extent, cuts, smallest, high):
    def one(dim, shards_of):
        draws = jax.random.uniform(jax.random.fold_in(jax.random.fold_in(stream_key, 6), dim), (shards_of,), jnp.float32, smallest / len(cuts), high / len(cuts))
        return jnp.repeat(jnp.exp(draws), extent[dim] // shards_of).reshape((-1,) + (1,) * (len(extent) - dim - 1))

    gain = one(*cuts[0])
    for cut in cuts[1:]:
        gain = gain * one(*cut)
    return gain


def normal_values(stream_key, shape, scale, reach, pieces=(), dtype=jnp.bfloat16):
    values = scale * jax.random.normal(stream_key, shape, jnp.float32)
    if pieces:
        values = values * level_of(stream_key, shape, pieces, -0.22, 0.18)
    return jnp.clip(values, -reach, reach).astype(dtype)


def setup_inputs(seed: int = 0, part: int = 0) -> dict:
    key_of = jax.random.split(jax.random.key(seed), 11)
    own_keys = jax.random.split(jax.random.fold_in(key_of[10], part), 11)
    field = normal_values(own_keys[0], (2, R, NA, Z), 1.0, 6.0, ((2, 16),), jnp.float32)
    source = normal_values(own_keys[1], (2, R, NA, Z), 1.0, 6.0, ((2, 16),), jnp.float32)
    materials = with_ends(jax.random.randint(own_keys[2], (2, R, NA, Z), 0, MATS), jax.random.fold_in(own_keys[2], 1), 0, MATS - 1).astype(jnp.int32)
    incoming = normal_values(own_keys[3], (2, STEPS, NA, Z), 1.0, 6.0, ((2, 16),), jnp.float32)
    waveform = jnp.clip(jax.random.uniform(own_keys[4], (STEPS,), jnp.float32, -1.0, 1.0), -1.0, 1.0)
    degrees = draw_degrees(jax.random.fold_in(jax.random.fold_in(key_of[10], part), 71), part)
    offsets = with_ends(jax.random.randint(own_keys[6], (STEPS,), 0, SECTORS), jax.random.fold_in(own_keys[6], 1), 0, SECTORS - 1).astype(jnp.int32)
    conduct = jnp.clip(jnp.exp(jax.random.uniform(key_of[7], (MATS,), jnp.float32, math.log(0.05), math.log(0.5))), 0.05, 0.5)
    reluct = jnp.clip(jnp.exp(jax.random.uniform(key_of[8], (MATS,), jnp.float32, math.log(0.3), math.log(3.0))), 0.3, 3.0)
    robin = jnp.clip(jnp.exp(jax.random.uniform(key_of[9], (2,), jnp.float32, math.log(0.5), math.log(2.0))), 0.5, 2.0)
    return dict(field=field, source=source, materials=materials, incoming=incoming, waveform=waveform, degrees=degrees, offsets=offsets, conduct=conduct, reluct=reluct, robin=robin)


THETA = 1.05
DELTA = 0.95


def rates(count):
    rho = DELTA / THETA
    first = []
    second = []
    for step in range(count):
        fresh = 1.0 / (2.0 * THETA / DELTA - rho)
        first.append(fresh * rho)
        second.append(2.0 * fresh / DELTA)
        rho = fresh
    return first, second


def lookup(mats, table):
    result = jnp.zeros(mats.shape, jnp.float32)
    for index in range(table.shape[0]):
        result = result + jnp.where(mats == index, table[index], 0.0)
    return result


def centre(values, width):
    start = (values.shape[2] - width) // 2
    return values[:, :, start:start + width]


def coefs(nu_ext, sig, robin):
    nu_c = nu_ext[:, :, 1:-1]
    ka_p = 0.5 * (nu_c + nu_ext[:, :, 2:])
    ka_m = 0.5 * (nu_c + nu_ext[:, :, :-2])
    kr_in = 0.5 * (nu_c[:, :-1] + nu_c[:, 1:])
    zero_r = jnp.zeros_like(nu_c[:, :1])
    kr_p = jnp.concatenate([kr_in, zero_r], 1)
    kr_m = jnp.concatenate([zero_r, kr_in], 1)
    kz_in = 0.5 * (nu_c[..., :-1] + nu_c[..., 1:])
    zero_z = jnp.zeros_like(nu_c[..., :1])
    kz_p = jnp.concatenate([kz_in, zero_z], 3)
    kz_m = jnp.concatenate([zero_z, kz_in], 3)
    rpos = lax.broadcasted_iota(jnp.int32, nu_c.shape, 1)
    zpos = lax.broadcasted_iota(jnp.int32, nu_c.shape, 3)
    border = jnp.where(rpos == 0, nu_c, 0.0) + jnp.where(zpos == 0, nu_c, 0.0)
    border = border + jnp.where(zpos == nu_c.shape[3] - 1, nu_c, 0.0)
    border = border + jnp.where(rpos == nu_c.shape[1] - 1, robin[:, None, None, None], 0.0)
    diag = sig + ka_p + ka_m + kr_p + kr_m + kz_p + kz_m + border
    return (ka_p, ka_m, kr_p, kr_m, kz_p, kz_m, diag, 1.0 / diag)


def operate(x_ext, coef):
    ka_p, ka_m, kr_p, kr_m, kz_p, kz_m, diag, dinv = coef
    x_c = x_ext[:, :, 1:-1]
    zero_r = jnp.zeros_like(x_c[:, :1])
    zero_z = jnp.zeros_like(x_c[..., :1])
    up_r = jnp.concatenate([x_c[:, 1:], zero_r], 1)
    down_r = jnp.concatenate([zero_r, x_c[:, :-1]], 1)
    up_z = jnp.concatenate([x_c[..., 1:], zero_z], 3)
    down_z = jnp.concatenate([zero_z, x_c[..., :-1]], 3)
    beside = ka_p * x_ext[:, :, 2:] + ka_m * x_ext[:, :, :-2] + kr_p * up_r + kr_m * down_r
    beside = beside + kz_p * up_z + kz_m * down_z
    return diag * x_c - beside


def cycle(values, width):
    return jnp.concatenate([values[:, :, -width:], values, values[:, :, :width]], 2)


def reference(field, source, materials, incoming, waveform, degrees, offsets, conduct, reluct, robin):
    nu = lookup(materials, reluct)
    sig = lookup(materials, conduct)
    coef = coefs(cycle(nu, 1), sig, robin)
    first, second = rates(DEG)
    layer = field.shape[1] - 1
    state = field
    traces = []
    for step in range(STEPS):
        rhs = sig * state + waveform[step] * source
        rhs = rhs.at[:, layer].add(incoming[:, step])
        iterate = state
        resid = rhs - operate(cycle(iterate, 1), coef)
        direction = (coef[7] * resid) * (1.0 / THETA)
        for sweep in range(DEG):
            active = (sweep < degrees[step]).astype(jnp.float32)
            iterate = iterate + active * direction
            resid = resid - operate(cycle(direction, 1), coef)
            direction = first[sweep] * direction + second[sweep] * (coef[7] * resid)
        state = iterate
        traces.append(2.0 * robin[:, None, None] * state[:, layer] - incoming[:, step])
    rotor_new = []
    stator_new = []
    for step in range(STEPS):
        stator_new.append(jnp.roll(traces[step][0], offsets[step] * A_DEV, axis=0))
        rotor_new.append(jnp.roll(traces[step][1], -offsets[step] * A_DEV, axis=0))
    next_incoming = jnp.stack([jnp.stack(rotor_new), jnp.stack(stator_new)])
    return state, next_incoming
```

```python
import functools

import jax
import jax.numpy as jnp
from jax import lax
from jax.experimental import pallas as pl
from jax.experimental.pallas import tpu as pltpu
from jax.sharding import PartitionSpec as P

DEG = 8
THETA = 1.05
DELTA = 0.95
CHUNK = 4


def rates(count):
    rho = DELTA / THETA
    first = []
    second = []
    for step in range(count):
        fresh = 1.0 / (2.0 * THETA / DELTA - rho)
        first.append(fresh * rho)
        second.append(2.0 * fresh / DELTA)
        rho = fresh
    return (first, second)


def chunks(start, stop):
    return [(at, min(CHUNK, stop - at)) for at in range(start, stop, CHUNK)]


def kernel(
    count, cells, steps, radial, axial, mats,
    waveform, degrees, offsets, conduct, reluct, robin, packed,
    field_out, next_out,
    got, nu, sig, aplus, aminus, rplus, rminus, zplus, zminus, own, dsrc, dtop,
    state, resid, direct, staged,
    send_mat, recv_mat, send_rest, recv_rest, send_halo, recv_halo,
    send_trace, recv_trace, send_last, recv_last, *whole,
):
    chips = count // 2
    wide = 2 * cells
    ext = 3 * wide
    group = lax.axis_index("groups")
    place = lax.axis_index("sector")
    chip = lax.div(place, 2)
    core = lax.rem(place, 2)
    other = 1 - core

    def device(to_chip, to_core):
        return {"groups": group, "sector": 2 * to_chip + to_core}

    def away(distance):
        return lax.rem(chip + distance + chips, chips)

    def copy(src, dst, send, recv, target):
        return pltpu.make_async_remote_copy(
            src_ref=src, dst_ref=dst, send_sem=send, recv_sem=recv,
            device_id=target, device_id_type=pl.DeviceIdType.MESH,
        )

    barrier = pltpu.get_barrier_semaphore()
    partners = [device(away(d), core) for d in range(1, chips)]
    partners += [device(away(d), other) for d in (-1, 0, 1)]
    for target in partners:
        pl.semaphore_signal(barrier, inc=1, device_id=target, device_id_type=pl.DeviceIdType.MESH)
    got[1, core] = packed[core]
    pl.semaphore_wait(barrier, len(partners))

    tiles = packed.shape[1]
    moves = []
    for part, send, recv in (((0, cells), send_mat, recv_mat), ((cells, tiles - cells), send_rest, recv_rest)):
        first, size = part
        line = []
        for d, flip in ((-1, 0), (1, 0), (-1, 1), (1, 1), (0, 1)):
            to_core = other if flip else core
            line.append(copy(
                packed.at[to_core, pl.ds(first, size)],
                got.at[1 - d, core, pl.ds(first, size)],
                send.at[1 + d, flip], recv.at[1 - d, core],
                device(away(d), to_core),
            ))
        for move in line:
            move.start()
        moves.append(line)

    def arrive(recv, first, size):
        for d, flip in ((-1, 0), (1, 0), (-1, 1), (1, 1), (0, 1)):
            from_core = other if flip else core
            copy(
                packed.at[core, pl.ds(first, size)],
                got.at[1 + d, from_core, pl.ds(first, size)],
                send_mat.at[0, 0], recv.at[1 + d, from_core],
                device(away(d), from_core),
            ).wait_recv()

    def block(cell):
        return cell // wide, (cell // cells) % 2, cell % cells

    arrive(recv_mat, 0, cells)
    rob = robin[core]
    for a in range(0, ext, cells):
        i, k, _ = block(a)
        kind = got[i, k, 0:cells]
        nu_new = jnp.zeros(kind.shape, jnp.float32)
        sig_new = jnp.zeros(kind.shape, jnp.float32)
        for index in range(mats):
            hit = kind == float(index)
            nu_new = nu_new + jnp.where(hit, reluct[index], 0.0)
            sig_new = sig_new + jnp.where(hit, conduct[index], 0.0)
        nu[a : a + cells] = nu_new
        sig[a : a + cells] = sig_new
    for a, n in chunks(1, ext - 1):
        shape = (n, radial, axial)
        rpos = lax.broadcasted_iota(jnp.int32, shape, 1)
        zpos = lax.broadcasted_iota(jnp.int32, shape, 2)
        here = nu[a : a + n]
        cond = sig[a : a + n]
        kap = 0.5 * (here + nu[a + 1 : a + n + 1])
        kam = 0.5 * (here + nu[a - 1 : a + n - 1])
        low, top = rpos == 0, rpos == radial - 1
        front, back = zpos == 0, zpos == axial - 1
        krp = jnp.where(top, 0.0, 0.5 * (here + pltpu.roll(here, radial - 1, 1)))
        krm = jnp.where(low, 0.0, 0.5 * (here + pltpu.roll(here, 1, 1)))
        kzp = jnp.where(back, 0.0, 0.5 * (here + pltpu.roll(here, axial - 1, 2)))
        kzm = jnp.where(front, 0.0, 0.5 * (here + pltpu.roll(here, 1, 2)))
        border = jnp.where(low, here, 0.0) + jnp.where(front, here, 0.0)
        border = border + jnp.where(back, here, 0.0) + jnp.where(top, rob, 0.0)
        diag = cond + kap + kam + krp + krm + kzp + kzm + border
        dinv = 1.0 / diag
        aplus[a : a + n] = dinv * kap
        aminus[a : a + n] = dinv * kam
        rplus[a : a + n] = dinv * krp
        rminus[a : a + n] = dinv * krm
        zplus[a : a + n] = dinv * kzp
        zminus[a : a + n] = dinv * kzm
        own[a : a + n] = dinv * cond - 1.0
        dtop[a : a + n] = jnp.where(top, dinv, 0.0)
        dsrc[a : a + n] = dinv
    arrive(recv_rest, cells, tiles - cells)
    for a in range(0, ext, cells):
        i, k, _ = block(a)
        state[0, a : a + cells] = got[i, k, cells : 2 * cells]
    for a, n in chunks(1, ext - 1):
        for cell in range(a, a + n):
            i, k, j = block(cell)
            dsrc[cell] = dsrc[cell] * got[i, k, 2 * cells + j]

    def given(cell, step):
        i, k, j = block(cell)
        row = j * steps + step
        return got[i, k, 3 * cells + row // radial, row % radial : row % radial + 1, :]

    def beside(src, a, n):
        mid = src[a : a + n]
        total = aplus[a : a + n] * src[a + 1 : a + n + 1]
        total = total + aminus[a : a + n] * src[a - 1 : a + n - 1]
        total = total + rplus[a : a + n] * pltpu.roll(mid, radial - 1, 1)
        total = total + rminus[a : a + n] * pltpu.roll(mid, 1, 1)
        total = total + zplus[a : a + n] * pltpu.roll(mid, axial - 1, 2)
        total = total + zminus[a : a + n] * pltpu.roll(mid, 1, 2)
        return mid, total

    first, second = rates(DEG)
    halo_moves = []
    trace_moves = []
    for step in range(steps):
        if step > 0:
            for line in halo_moves[-1]:
                line.wait_recv()
        here = state.at[step]
        wave = waveform[step]
        degree = degrees[step]
        for a, n in chunks(1, ext - 1):
            mid, total = beside(here, a, n)
            extra = jnp.stack([jnp.broadcast_to(given(cell, step), (radial, axial)) for cell in range(a, a + n)])
            fresh = total + own[a : a + n] * mid + wave * dsrc[a : a + n]
            fresh = fresh + dtop[a : a + n] * extra
            resid[a : a + n] = fresh
            direct[0, a : a + n] = fresh * (1.0 / THETA)
        for sweep in range(DEG):
            active = (sweep < degree).astype(jnp.float32)
            old = direct.at[sweep % 2]
            new = direct.at[(sweep + 1) % 2]
            base = here if sweep == 0 else state.at[step + 1]
            for a, n in chunks(wide, 2 * wide):
                state[step + 1, a : a + n] = base[a : a + n] + active * old[a : a + n]
            if sweep == DEG - 1:
                break
            for a, n in chunks(2 + sweep, ext - 2 - sweep):
                mid, total = beside(old, a, n)
                fresh = resid[a : a + n] - mid + total
                resid[a : a + n] = fresh
                new[a : a + n] = first[sweep] * mid + second[sweep] * fresh
        after = state.at[step + 1]
        if step < steps - 1:
            line = [
                copy(
                    after.at[pl.ds(wide, wide)], after.at[pl.ds((1 - d) * wide, wide)],
                    send_halo.at[step, (d + 1) // 2], recv_halo.at[step, (d + 1) // 2],
                    device(away(d), core),
                )
                for d in (-1, 1)
            ]
            for move in line:
                move.start()
            halo_moves.append(line)
        for cell in range(wide):
            trace = 2.0 * rob * after[wide + cell, radial - 1 : radial, :] - given(wide + cell, step)
            whole[step][chip, cell // cells, cell % cells : cell % cells + 1, :] = trace
        for d in range(1, chips):
            move = copy(
                whole[step].at[chip], whole[step].at[chip],
                send_trace.at[step, d], recv_trace.at[step, d], device(away(d), core),
            )
            move.start()
            trace_moves.append(move)

    last = state.at[steps]
    swap = copy(
        last.at[pl.ds(wide + cells * other, cells)], field_out.at[core],
        send_last.at[0], recv_last.at[0], device(chip, other),
    )
    swap.start()
    field_out[core] = last[pl.ds(wide + cells * core, cells)]
    sign = 2 * core - 1
    for step in range(steps):
        for d in range(1, chips):
            trace_moves[step * (chips - 1) + d - 1].wait_recv()
        shift = sign * offsets[step] + count
        near = lax.rem(place + shift, count)
        far = lax.rem(2 * chip + other + shift, count)
        next_out[other, step] = whole[step][lax.div(near, 2), lax.rem(near, 2)]
        staged[step] = whole[step][lax.div(far, 2), lax.rem(far, 2)]
    swap_next = copy(
        staged, next_out.at[other], send_last.at[1], recv_last.at[1], device(chip, other),
    )
    swap_next.start()
    for line in moves:
        for move in line:
            move.wait_send()
    for line in halo_moves:
        for move in line:
            move.wait_send()
    for move in trace_moves:
        move.wait_send()
    swap.wait()
    swap_next.wait()


def per_device(
    count, field, source, materials, incoming, waveform, degrees, offsets, conduct, reluct, robin
):
    regions, radial, cells, axial = field.shape
    steps = incoming.shape[1]
    chips = count // 2
    turned = [
        jnp.transpose(v, (0, 2, 1, 3)) for v in (materials.astype(jnp.float32), field, source)
    ]
    given = jnp.transpose(incoming, (0, 2, 1, 3)).reshape(regions, -1, radial, axial)
    packed = jnp.concatenate(turned + [given], axis=1)
    tiles = packed.shape[1]
    ext = 6 * cells
    vmem = pl.BlockSpec(memory_space=pltpu.VMEM)
    smem = pl.BlockSpec(memory_space=pltpu.SMEM)

    def area(*lead):
        return pltpu.VMEM((*lead, radial, axial), jnp.float32)

    dma = pltpu.SemaphoreType.DMA
    field_end, next_incoming = pl.pallas_call(
        functools.partial(kernel, count, cells, steps, radial, axial, conduct.shape[0]),
        out_shape=(
            jax.ShapeDtypeStruct((regions, cells, radial, axial), jnp.float32),
            jax.ShapeDtypeStruct((regions, steps, cells, axial), jnp.float32),
        ),
        in_specs=[smem] * 6 + [vmem],
        out_specs=(vmem, vmem),
        scratch_shapes=[
            area(3, 2, tiles),
            *[area(ext) for _ in range(11)],
            area(steps + 1, ext),
            area(ext),
            area(2, ext),
            pltpu.VMEM((steps, cells, axial), jnp.float32),
            dma((3, 2)),
            dma((3, 2)),
            dma((3, 2)),
            dma((3, 2)),
            dma((steps, 2)),
            dma((steps, 2)),
            dma((steps, chips)),
            dma((steps, chips)),
            dma((2,)),
            dma((2,)),
            *[pltpu.VMEM((chips, 2, cells, axial), jnp.float32) for _ in range(steps)],
        ],
        compiler_params=pltpu.CompilerParams(
            collective_id=0, has_side_effects=True, vmem_limit_bytes=32 * 1024 * 1024
        ),
        name="window",
    )(waveform, degrees, offsets, conduct, reluct, robin, packed)
    return (jnp.transpose(field_end, (0, 2, 1, 3)), next_incoming)


def solution(mesh):
    return jax.shard_map(
        functools.partial(per_device, mesh.shape["sector"]),
        mesh=mesh,
        in_specs=(
            P("groups", None, "sector", None),
            P("groups", None, "sector", None),
            P("groups", None, "sector", None),
            P("groups", None, "sector", None),
            P("groups"),
            P("groups"),
            P("groups"),
            P(),
            P(),
            P(),
        ),
        out_specs=(P("groups", None, "sector", None), P("groups", None, "sector", None)),
        check_vma=False,
    )
```

```python
import functools

import jax
import jax.numpy as jnp
from jax import lax
from jax.experimental import pallas as pl
from jax.experimental.pallas import tpu as pltpu
from jax.sharding import PartitionSpec as P

DEG = 8
THETA = 1.05
DELTA = 0.95
CHUNK = 4


def rates(count):
    rho = DELTA / THETA
    first = []
    second = []
    for step in range(count):
        fresh = 1.0 / (2.0 * THETA / DELTA - rho)
        first.append(fresh * rho)
        second.append(2.0 * fresh / DELTA)
        rho = fresh
    return (first, second)


def chunks(start, stop):
    return [(at, min(CHUNK, stop - at)) for at in range(start, stop, CHUNK)]


def kernel(
    count, cells, steps, radial, axial, mats,
    waveform, degrees, offsets, conduct, reluct, robin, packed,
    field_out, next_out,
    got, nu, sig, aplus, aminus, rplus, rminus, zplus, zminus, own, dsrc, dtop,
    state, resid, direct, staged,
    send_mat, recv_mat, send_rest, recv_rest, send_halo, recv_halo,
    send_trace, recv_trace, send_last, recv_last, *whole,
):
    chips = count // 2
    wide = 2 * cells
    ext = 3 * wide
    group = lax.axis_index("groups")
    place = lax.axis_index("sector")
    half = lax.rem(place, 2)
    home = lax.div(place, 2)
    chip = 2 * lax.div(place, 4) + half
    core = lax.rem(home, 2)
    other = 1 - core

    def device(to_chip, to_core):
        return at(sector_of(to_chip, to_core))

    def sector_of(to_chip, to_core):
        return 4 * lax.div(to_chip, 2) + 2 * to_core + lax.rem(to_chip, 2)

    def at(sector):
        return {"groups": group, "sector": sector}

    def away(distance):
        return lax.rem(chip + distance + chips, chips)

    def copy(src, dst, send, recv, target):
        return pltpu.make_async_remote_copy(
            src_ref=src, dst_ref=dst, send_sem=send, recv_sem=recv,
            device_id=target, device_id_type=pl.DeviceIdType.MESH,
        )

    barrier = pltpu.get_barrier_semaphore()
    partners = [at(lax.rem(place + d, count)) for d in range(1, count)]
    for target in partners:
        pl.semaphore_signal(barrier, inc=1, device_id=target, device_id_type=pl.DeviceIdType.MESH)
    got[1 + home - chip, half] = packed[core]
    pl.semaphore_wait(barrier, len(partners))

    tiles = packed.shape[1]
    parts = ((0, cells, send_mat, recv_mat), (cells, tiles - cells, send_rest, recv_rest))

    def ship(part, begin):
        first, size, send, recv = part
        for d in (-1, 1, 0):
            block_to = lax.rem(home + d + chips, chips)
            for region in (0, 1):
                target = sector_of(block_to, region)

                @pl.when(target != place)
                def _():
                    move = copy(
                        packed.at[region, pl.ds(first, size)],
                        got.at[1 - d, half, pl.ds(first, size)],
                        send.at[1 + d, region], recv.at[1 - d, half], at(target),
                    )
                    if begin:
                        move.start()
                    else:
                        move.wait_send()

    for part in parts:
        ship(part, True)

    def arrive(part):
        first, size, send, recv = part
        for d in (-1, 1, 0):
            for k in (0, 1):
                source = 2 * away(d) + k

                @pl.when(source != place)
                def _():
                    copy(
                        packed.at[0, pl.ds(first, size)],
                        got.at[1 + d, k, pl.ds(first, size)],
                        send.at[0, 0], recv.at[1 + d, k], at(source),
                    ).wait_recv()

    def block(cell):
        return cell // wide, (cell // cells) % 2, cell % cells

    arrive(parts[0])
    rob = robin[core]
    for a in range(0, ext, cells):
        i, k, _ = block(a)
        kind = got[i, k, 0:cells]
        nu_new = jnp.zeros(kind.shape, jnp.float32)
        sig_new = jnp.zeros(kind.shape, jnp.float32)
        for index in range(mats):
            hit = kind == float(index)
            nu_new = nu_new + jnp.where(hit, reluct[index], 0.0)
            sig_new = sig_new + jnp.where(hit, conduct[index], 0.0)
        nu[a : a + cells] = nu_new
        sig[a : a + cells] = sig_new
    for a, n in chunks(1, ext - 1):
        shape = (n, radial, axial)
        rpos = lax.broadcasted_iota(jnp.int32, shape, 1)
        zpos = lax.broadcasted_iota(jnp.int32, shape, 2)
        here = nu[a : a + n]
        cond = sig[a : a + n]
        kap = 0.5 * (here + nu[a + 1 : a + n + 1])
        kam = 0.5 * (here + nu[a - 1 : a + n - 1])
        low, top = rpos == 0, rpos == radial - 1
        front, back = zpos == 0, zpos == axial - 1
        krp = jnp.where(top, 0.0, 0.5 * (here + pltpu.roll(here, radial - 1, 1)))
        krm = jnp.where(low, 0.0, 0.5 * (here + pltpu.roll(here, 1, 1)))
        kzp = jnp.where(back, 0.0, 0.5 * (here + pltpu.roll(here, axial - 1, 2)))
        kzm = jnp.where(front, 0.0, 0.5 * (here + pltpu.roll(here, 1, 2)))
        border = jnp.where(low, here, 0.0) + jnp.where(front, here, 0.0)
        border = border + jnp.where(back, here, 0.0) + jnp.where(top, rob, 0.0)
        diag = cond + kap + kam + krp + krm + kzp + kzm + border
        dinv = 1.0 / diag
        aplus[a : a + n] = dinv * kap
        aminus[a : a + n] = dinv * kam
        rplus[a : a + n] = dinv * krp
        rminus[a : a + n] = dinv * krm
        zplus[a : a + n] = dinv * kzp
        zminus[a : a + n] = dinv * kzm
        own[a : a + n] = dinv * cond - 1.0
        dtop[a : a + n] = jnp.where(top, dinv, 0.0)
        dsrc[a : a + n] = dinv
    arrive(parts[1])
    for a in range(0, ext, cells):
        i, k, _ = block(a)
        state[0, a : a + cells] = got[i, k, cells : 2 * cells]
    for a, n in chunks(1, ext - 1):
        for cell in range(a, a + n):
            i, k, j = block(cell)
            dsrc[cell] = dsrc[cell] * got[i, k, 2 * cells + j]

    def given(cell, step):
        i, k, j = block(cell)
        row = j * steps + step
        return got[i, k, 3 * cells + row // radial, row % radial : row % radial + 1, :]

    def beside(src, a, n):
        mid = src[a : a + n]
        total = aplus[a : a + n] * src[a + 1 : a + n + 1]
        total = total + aminus[a : a + n] * src[a - 1 : a + n - 1]
        total = total + rplus[a : a + n] * pltpu.roll(mid, radial - 1, 1)
        total = total + rminus[a : a + n] * pltpu.roll(mid, 1, 1)
        total = total + zplus[a : a + n] * pltpu.roll(mid, axial - 1, 2)
        total = total + zminus[a : a + n] * pltpu.roll(mid, 1, 2)
        return mid, total

    first, second = rates(DEG)
    halo_moves = []
    trace_moves = []
    for step in range(steps):
        if step > 0:
            for line in halo_moves[-1]:
                line.wait_recv()
        here = state.at[step]
        wave = waveform[step]
        degree = degrees[step]
        for a, n in chunks(1, ext - 1):
            mid, total = beside(here, a, n)
            extra = jnp.stack([jnp.broadcast_to(given(cell, step), (radial, axial)) for cell in range(a, a + n)])
            fresh = total + own[a : a + n] * mid + wave * dsrc[a : a + n]
            fresh = fresh + dtop[a : a + n] * extra
            resid[a : a + n] = fresh
            direct[0, a : a + n] = fresh * (1.0 / THETA)
        for sweep in range(DEG):
            active = (sweep < degree).astype(jnp.float32)
            old = direct.at[sweep % 2]
            new = direct.at[(sweep + 1) % 2]
            base = here if sweep == 0 else state.at[step + 1]
            for a, n in chunks(wide, 2 * wide):
                state[step + 1, a : a + n] = base[a : a + n] + active * old[a : a + n]
            if sweep == DEG - 1:
                break
            for a, n in chunks(2 + sweep, ext - 2 - sweep):
                mid, total = beside(old, a, n)
                fresh = resid[a : a + n] - mid + total
                resid[a : a + n] = fresh
                new[a : a + n] = first[sweep] * mid + second[sweep] * fresh
        after = state.at[step + 1]
        if step < steps - 1:
            line = [
                copy(
                    after.at[pl.ds(wide, wide)], after.at[pl.ds((1 - d) * wide, wide)],
                    send_halo.at[step, (d + 1) // 2], recv_halo.at[step, (d + 1) // 2],
                    device(away(d), core),
                )
                for d in (-1, 1)
            ]
            for move in line:
                move.start()
            halo_moves.append(line)
        for cell in range(wide):
            trace = 2.0 * rob * after[wide + cell, radial - 1 : radial, :] - given(wide + cell, step)
            whole[step][chip, cell // cells, cell % cells : cell % cells + 1, :] = trace
        for d in range(1, chips):
            move = copy(
                whole[step].at[chip], whole[step].at[chip],
                send_trace.at[step, d], recv_trace.at[step, d], device(away(d), core),
            )
            move.start()
            trace_moves.append(move)

    last = state.at[steps]

    def hand(kind, k, begin):
        target = 2 * chip + k

        @pl.when(target != place)
        def _():
            move = copy(
                last.at[pl.ds(wide + cells * k, cells)] if kind == 0 else staged.at[k],
                field_out.at[core] if kind == 0 else next_out.at[other],
                send_last.at[kind, k], recv_last.at[kind, core], at(target),
            )
            if begin:
                move.start()
            else:
                move.wait_send()

        if begin:
            @pl.when(target == place)
            def _():
                if kind == 0:
                    field_out[core] = last[wide + cells * k : wide + cells * k + cells]
                else:
                    next_out[other] = staged[k]

    def take(kind, region):
        source = sector_of(home, region)

        @pl.when(source != place)
        def _():
            copy(
                last.at[pl.ds(wide, cells)] if kind == 0 else staged.at[0],
                field_out.at[region] if kind == 0 else next_out.at[1 - region],
                send_last.at[kind, 0], recv_last.at[kind, region], at(source),
            ).wait_recv()

    for k in (0, 1):
        hand(0, k, True)
    sign = 2 * core - 1
    for step in range(steps):
        for d in range(1, chips):
            trace_moves[step * (chips - 1) + d - 1].wait_recv()
        shift = sign * offsets[step] + count
        for k in (0, 1):
            near = lax.rem(2 * chip + k + shift, count)
            staged[k, step] = whole[step][lax.div(near, 2), lax.rem(near, 2)]
    for k in (0, 1):
        hand(1, k, True)
    for part in parts:
        ship(part, False)
    for line in halo_moves:
        for move in line:
            move.wait_send()
    for move in trace_moves:
        move.wait_send()
    for kind in (0, 1):
        for k in (0, 1):
            hand(kind, k, False)
            take(kind, k)


def per_device(
    count, field, source, materials, incoming, waveform, degrees, offsets, conduct, reluct, robin
):
    regions, radial, cells, axial = field.shape
    steps = incoming.shape[1]
    chips = count // 2
    turned = [
        jnp.transpose(v, (0, 2, 1, 3)) for v in (materials.astype(jnp.float32), field, source)
    ]
    given = jnp.transpose(incoming, (0, 2, 1, 3)).reshape(regions, -1, radial, axial)
    packed = jnp.concatenate(turned + [given], axis=1)
    tiles = packed.shape[1]
    ext = 6 * cells
    vmem = pl.BlockSpec(memory_space=pltpu.VMEM)
    smem = pl.BlockSpec(memory_space=pltpu.SMEM)

    def area(*lead):
        return pltpu.VMEM((*lead, radial, axial), jnp.float32)

    dma = pltpu.SemaphoreType.DMA
    field_end, next_incoming = pl.pallas_call(
        functools.partial(kernel, count, cells, steps, radial, axial, conduct.shape[0]),
        out_shape=(
            jax.ShapeDtypeStruct((regions, cells, radial, axial), jnp.float32),
            jax.ShapeDtypeStruct((regions, steps, cells, axial), jnp.float32),
        ),
        in_specs=[smem] * 6 + [vmem],
        out_specs=(vmem, vmem),
        scratch_shapes=[
            area(3, 2, tiles),
            *[area(ext) for _ in range(11)],
            area(steps + 1, ext),
            area(ext),
            area(2, ext),
            pltpu.VMEM((2, steps, cells, axial), jnp.float32),
            dma((3, 2)),
            dma((3, 2)),
            dma((3, 2)),
            dma((3, 2)),
            dma((steps, 2)),
            dma((steps, 2)),
            dma((steps, chips)),
            dma((steps, chips)),
            dma((2, 2)),
            dma((2, 2)),
            *[pltpu.VMEM((chips, 2, cells, axial), jnp.float32) for _ in range(steps)],
        ],
        compiler_params=pltpu.CompilerParams(
            collective_id=0, has_side_effects=True, vmem_limit_bytes=32 * 1024 * 1024
        ),
        name="window",
    )(waveform, degrees, offsets, conduct, reluct, robin, packed)
    return (jnp.transpose(field_end, (0, 2, 1, 3)), next_incoming)


def solution(mesh):
    return jax.shard_map(
        functools.partial(per_device, mesh.shape["sector"]),
        mesh=mesh,
        in_specs=(
            P("groups", None, "sector", None),
            P("groups", None, "sector", None),
            P("groups", None, "sector", None),
            P("groups", None, "sector", None),
            P("groups"),
            P("groups"),
            P("groups"),
            P(),
            P(),
            P(),
        ),
        out_specs=(P("groups", None, "sector", None), P("groups", None, "sector", None)),
        check_vma=False,
    )
```
